32 devices in a mesh: section: 16 (over z, y, core), tp: 2 (over x).
Axes of the slice: x: 2, y: 2, z: 4, core: 2. Of those that a mesh axis runs over, the one named last changes fastest.
Arguments:
- query_key_value_weight: bfloat16 [16, 2048, 3, 2048], P('section', None, None, 'tp'), may hold values from -6 to 6
- output_weight: bfloat16 [16, 2048, 2048], P('section', 'tp'), may hold values from -0.125 to 0.125
- ascending_query_key_value_weight: bfloat16 [16, 2048, 3, 2048], P('section', None, None, 'tp'), may hold values from -6 to 6
- ascending_output_weight: bfloat16 [16, 2048, 2048], P('section', 'tp'), may hold values from -0.125 to 0.125
- descending_saved_input: bfloat16 [16, 3, 128, 2048], P('section', None, 'tp'), may hold values from -6 to 6
- ascending_saved_input: bfloat16 [16, 3, 128, 2048], P('section', None, 'tp'), may hold values from -6 to 6
- descending_transit_gradient: bfloat16 [16, 128, 2048], P('section', 'tp'), may hold values from -4 to 4
- ascending_transit_gradient: bfloat16 [16, 128, 2048], P('section', 'tp'), may hold values from -4 to 4
- descending_loss_gradient: bfloat16 [2, 128, 2048], P(None, 'tp'), may hold values from -4 to 4
- ascending_loss_gradient: bfloat16 [2, 128, 2048], P(None, 'tp'), may hold values from -4 to 4
Outputs:
- grad_qkv: bfloat16 [16, 2048, 3, 2048], P('section', None, None, 'tp')
- grad_out: bfloat16 [16, 2048, 2048], P('section', 'tp')
- final_down: bfloat16 [16, 128, 2048], P('section', 'tp')
- final_up: bfloat16 [16, 128, 2048], P('section', 'tp')
The draws below stay inside these ranges and needn't reach their ends.
All inputs are finite; a program needn't handle non-finite values.
Results may differ from the reference program's by a relative error of at most 0.029.
Values may be sent and summed in bfloat16 or wider, within the bound.
A program may use at most 320 MiB of HBM per device.

```python
import jax
import jax.numpy as jnp
from jax import lax

MODEL_WIDTH = 2048
HEADS = 16
HEAD = 128
MICRO_TOKENS = 128
TICKS = 3
HD = 2048
LAYER_COUNT = 16


def drawn_qkv(normal_key):
    return jnp.clip(jax.random.normal(normal_key, (LAYER_COUNT, MODEL_WIDTH, 3, HD), jnp.float32), -6.0, 6.0) * MODEL_WIDTH ** (-0.5)


def draw_query_key_value_weight(key, part):
    key = jax.random.fold_in(key, 7)
    normal_key = jax.random.fold_in(key, 0)
    drawn = drawn_qkv(normal_key)
    return drawn.astype(jnp.bfloat16)


def draw_ascending_query_key_value_weight(key, part):
    key = jax.random.fold_in(key, 11)
    normal_key = jax.random.fold_in(key, 0)
    drawn = drawn_qkv(normal_key)
    return drawn.astype(jnp.bfloat16)


def block_scale(stream_key, dims, cuts, least, top_value):
    level = 1.0
    for position, shards_of in cuts:
        heights = jax.random.uniform(jax.random.fold_in(jax.random.fold_in(stream_key, 6), position), (shards_of,), jnp.float32, least / len(cuts), top_value / len(cuts))
        level = level * jnp.repeat(jnp.exp(heights), dims[position] // shards_of).reshape((-1,) + (1,) * (len(dims) - 1 - position))
    return level


def centred(rng, shape, scale, most, shards=(), dtype=jnp.bfloat16):
    values = jax.random.normal(rng, shape, jnp.float32) * scale
    if len(shards) > 0:
        values = block_scale(rng, shape, shards, -0.22, 0.18) * values
    return jnp.clip(values, min=-most, max=most).astype(dtype)


def setup_inputs(seed: int = 0) -> dict:
    key_of = jax.random.split(jax.random.key(seed), 11)
    return {
        "query_key_value_weight": draw_query_key_value_weight(jax.random.fold_in(key_of[10], 71), 0),
        "output_weight": centred(key_of[1], (LAYER_COUNT, HD, MODEL_WIDTH), HD ** -0.5, 0.125, ((0, 16), (1, 2))),
        "ascending_query_key_value_weight": draw_ascending_query_key_value_weight(jax.random.fold_in(key_of[10], 71), 0),
        "ascending_output_weight": centred(key_of[3], (LAYER_COUNT, HD, MODEL_WIDTH), HD ** -0.5, 0.125, ((0, 16), (1, 2))),
        "descending_saved_input": centred(key_of[4], (LAYER_COUNT, TICKS, MICRO_TOKENS, MODEL_WIDTH), 1.0, 6.0, ((0, 16), (2, 2))),
        "ascending_saved_input": centred(key_of[5], (LAYER_COUNT, TICKS, MICRO_TOKENS, MODEL_WIDTH), 1.0, 6.0, ((0, 16), (2, 2))),
        "descending_transit_gradient": centred(key_of[6], (LAYER_COUNT, MICRO_TOKENS, MODEL_WIDTH), 0.3, 4.0, ((0, 16), (1, 2))),
        "ascending_transit_gradient": centred(key_of[7], (LAYER_COUNT, MICRO_TOKENS, MODEL_WIDTH), 0.3, 4.0, ((0, 16), (1, 2))),
        "descending_loss_gradient": centred(key_of[8], (TICKS - 1, MICRO_TOKENS, MODEL_WIDTH), 0.3, 4.0, ((1, 2),)),
        "ascending_loss_gradient": centred(key_of[9], (TICKS - 1, MICRO_TOKENS, MODEL_WIDTH), 0.3, 4.0, ((1, 2),)),
    }


EPSILON = 1e-05

def layer_step(weights_qkv, weights_out, stored, upstream):
    score_scale = HEAD ** (-0.5)
    raw = stored.astype(jnp.float32)
    centre = raw - lax.optimization_barrier(jnp.mean(raw, axis=-1, keepdims=True))
    inverse = lax.rsqrt(lax.optimization_barrier(jnp.mean(centre * centre, axis=-1, keepdims=True)) + EPSILON)
    normed = centre * inverse
    hidden = normed.astype(jnp.bfloat16)
    flat_qkv = weights_qkv.reshape(MODEL_WIDTH, 3 * HD)
    project = jnp.dot(hidden, flat_qkv, preferred_element_type=jnp.float32).astype(jnp.bfloat16)
    project = project.reshape(MICRO_TOKENS, 3, HEADS, HEAD)
    queries = project[:, 0].astype(jnp.float32)
    key_rows = project[:, 1].astype(jnp.float32)
    value_rows = project[:, 2].astype(jnp.float32)
    scores = jnp.einsum('qhe,khe->hqk', queries, key_rows, precision=lax.Precision.HIGHEST) * score_scale
    causal = lax.broadcasted_iota(jnp.int32, (MICRO_TOKENS, MICRO_TOKENS), 0) >= lax.broadcasted_iota(jnp.int32, (MICRO_TOKENS, MICRO_TOKENS), 1)
    weights_soft = jax.nn.softmax(jnp.where(causal, scores, -jnp.inf), axis=-1)
    soft_half = weights_soft.astype(jnp.bfloat16).astype(jnp.float32)
    attended = jnp.einsum('hqk,khe->qhe', soft_half, value_rows, precision=lax.Precision.HIGHEST).astype(jnp.bfloat16)
    grad_out = jnp.dot(attended.reshape(MICRO_TOKENS, HD).T, upstream, preferred_element_type=jnp.float32)
    d_attended = jnp.dot(upstream, weights_out.T, preferred_element_type=jnp.float32).astype(jnp.bfloat16)
    d_attended = d_attended.reshape(MICRO_TOKENS, HEADS, HEAD).astype(jnp.float32)
    d_values = jnp.einsum('hqk,qhe->khe', soft_half, d_attended, precision=lax.Precision.HIGHEST).astype(jnp.bfloat16)
    d_probs = jnp.einsum('qhe,khe->hqk', d_attended, value_rows, precision=lax.Precision.HIGHEST)
    offset = jnp.einsum('qhe,qhe->hq', d_attended, attended.astype(jnp.float32), precision=lax.Precision.HIGHEST)
    d_scores = (weights_soft * (d_probs - offset[:, :, None]) * score_scale).astype(jnp.bfloat16).astype(jnp.float32)
    d_queries = jnp.einsum('hqk,khe->qhe', d_scores, key_rows, precision=lax.Precision.HIGHEST).astype(jnp.bfloat16)
    d_keys = jnp.einsum('hqk,qhe->khe', d_scores, queries, precision=lax.Precision.HIGHEST).astype(jnp.bfloat16)
    d_project = jnp.stack([d_queries, d_keys, d_values], axis=1).reshape(MICRO_TOKENS, 3 * HD)
    grad_qkv = jnp.dot(hidden.T, d_project, preferred_element_type=jnp.float32).reshape(MODEL_WIDTH, 3, HD)
    d_hidden = jnp.dot(d_project, flat_qkv.T, preferred_element_type=jnp.float32)
    backward = inverse * (d_hidden - lax.optimization_barrier(jnp.mean(d_hidden, axis=-1, keepdims=True)) - normed * lax.optimization_barrier(jnp.mean(d_hidden * normed, axis=-1, keepdims=True)))
    departing_gradient = (upstream.astype(jnp.float32) + backward).astype(jnp.bfloat16)
    return (departing_gradient, grad_qkv, grad_out)

def execute_relay_backward(query_key_value_weight, output_weight, saved_layer_input, transit_gradient, loss_gradient):
    arriving_gradient = transit_gradient
    sum_qkv = jnp.zeros((LAYER_COUNT, MODEL_WIDTH, 3, HD), jnp.float32)
    sum_out = jnp.zeros((LAYER_COUNT, HD, MODEL_WIDTH), jnp.float32)
    departing_gradient = transit_gradient
    for tick_index in range(TICKS):

        def one_layer(packed):
            weights_qkv, weights_out, stored, upstream, total_qkv, total_out = packed
            result, piece_qkv, piece_out = layer_step(weights_qkv, weights_out, stored, upstream)
            return (result, total_qkv + piece_qkv, total_out + piece_out)
        departing_gradient, sum_qkv, sum_out = lax.map(one_layer, (query_key_value_weight, output_weight, saved_layer_input[:, tick_index], arriving_gradient, sum_qkv, sum_out))
        if tick_index + 1 < TICKS:
            arriving_gradient = jnp.concatenate([departing_gradient[1:], loss_gradient[tick_index][None]], axis=0)
    return (departing_gradient, sum_qkv.astype(jnp.bfloat16), sum_out.astype(jnp.bfloat16))

def reference(query_key_value_weight, output_weight, ascending_query_key_value_weight, ascending_output_weight, descending_saved_input, ascending_saved_input, descending_transit_gradient, ascending_transit_gradient, descending_loss_gradient, ascending_loss_gradient):
    descending_final_layer, descending_query_key_value, descending_output_gradient = execute_relay_backward(query_key_value_weight, output_weight, descending_saved_input, descending_transit_gradient, descending_loss_gradient)
    ascending_final_section, ascending_query_key_value, ascending_output_gradient = execute_relay_backward(ascending_query_key_value_weight[::-1], ascending_output_weight[::-1], ascending_saved_input[::-1], ascending_transit_gradient[::-1], ascending_loss_gradient)
    grad_qkv = (descending_query_key_value.astype(jnp.float32) + ascending_query_key_value.astype(jnp.float32)).astype(jnp.bfloat16)
    grad_out = (descending_output_gradient.astype(jnp.float32) + ascending_output_gradient.astype(jnp.float32)).astype(jnp.bfloat16)
    return (grad_qkv, grad_out, descending_final_layer, ascending_final_section[::-1])
```

```python
import functools

import jax
import jax.numpy as jnp
from jax import lax
from jax.experimental import pallas as pl
from jax.experimental.pallas import tpu as pltpu
from jax.sharding import PartitionSpec as P

HEAD = 128
TICKS = 3
EPSILON = 1e-05
VMEM_BYTES = 48 * 1024 * 1024
NT = (((1,), (1,)), ((), ()))
TN = (((0,), (0,)), ((), ()))


def normalize(stored):
    raw = stored.astype(jnp.float32)
    centre = raw - jnp.mean(raw, axis=-1, keepdims=True)
    inverse = lax.rsqrt(jnp.mean(centre * centre, axis=-1, keepdims=True) + EPSILON)
    return (centre * inverse, inverse)


def layer_back(summed, normed, inverse, upstream):
    backward = inverse * (
        summed
        - jnp.mean(summed, axis=-1, keepdims=True)
        - normed * jnp.mean(summed * normed, axis=-1, keepdims=True)
    )
    return (upstream.astype(jnp.float32) + backward).astype(jnp.bfloat16)


def turned(value, shift):
    count = lax.axis_size("tp")
    return lax.ppermute(value, "tp", [(i, (i + shift) % count) for i in range(count)])


def gather_rows(value, axis):
    count = lax.axis_size("tp")
    blocks = [value] + [turned(value, k) for k in range(1, count)]
    return jnp.concatenate(blocks, axis=axis)


def scatter_rows(part):
    count = lax.axis_size("tp")
    rows = part.shape[0] // count
    total = part[:rows].astype(jnp.float32)
    for k in range(1, count):
        total = total + turned(part[k * rows : (k + 1) * rows], -k).astype(jnp.float32)
    return total


def passed_along(value, steps):
    sections, count = lax.axis_size("section"), lax.axis_size("tp")
    blocks = []
    for k in range(count):
        pairs = [
            (s * count + i, (s + steps) * count + (i + k) % count)
            for s in range(sections)
            if 0 <= s + steps < sections
            for i in range(count)
        ]
        blocks.append(lax.ppermute(value, ("section", "tp"), pairs))
    return jnp.concatenate(blocks, axis=0)


def mirror(value):
    sections = lax.axis_size("section")
    return lax.ppermute(value, "section", [(s, sections - 1 - s) for s in range(sections)])


def dot(a, b, dims=(((1,), (0,)), ((), ()))):
    return lax.dot_general(a, b, dims, preferred_element_type=jnp.float32)


def softmax_of(queries, keys, mask):
    scores = dot(queries, keys, NT) * HEAD ** (-0.5)
    scores = jnp.where(mask > 0.5, scores, -jnp.inf)
    raised = jnp.exp(scores - jnp.max(scores, axis=-1, keepdims=True))
    return raised / jnp.sum(raised, axis=-1, keepdims=True)


def forward_kernel(rows, hidden_ref, weight_ref, mask_ref, qkv_ref, attended_ref):
    hidden = hidden_ref[...]
    for c in range(3):
        qkv_ref[c] = dot(hidden, weight_ref[c]).astype(jnp.bfloat16)
    mask = mask_ref[...]
    for t in range(hidden.shape[0] // rows):
        r = pl.ds(t * rows, rows)
        for j in range(weight_ref.shape[2] // HEAD):
            e = pl.ds(j * HEAD, HEAD)
            soft = softmax_of(qkv_ref[0, r, e], qkv_ref[1, r, e], mask).astype(jnp.bfloat16)
            attended_ref[r, e] = dot(soft, qkv_ref[2, r, e]).astype(jnp.bfloat16)


def forward(hidden, weight, mask):
    all_rows, features = hidden.shape
    width = weight.shape[2]
    rows = mask.shape[0]
    block = 2 * HEAD if width % (2 * HEAD) == 0 else HEAD
    return pl.pallas_call(
        functools.partial(forward_kernel, rows),
        grid=(width // block,),
        in_specs=[
            pl.BlockSpec((all_rows, features), lambda j: (0, 0)),
            pl.BlockSpec((3, features, block), lambda j: (0, 0, j)),
            pl.BlockSpec((rows, rows), lambda j: (0, 0)),
        ],
        out_specs=[
            pl.BlockSpec((3, all_rows, block), lambda j: (0, 0, j)),
            pl.BlockSpec((all_rows, block), lambda j: (0, j)),
        ],
        out_shape=[
            jax.ShapeDtypeStruct((3, all_rows, width), jnp.bfloat16),
            jax.ShapeDtypeStruct((all_rows, width), jnp.bfloat16),
        ],
        compiler_params=pltpu.CompilerParams(vmem_limit_bytes=VMEM_BYTES),
        cost_estimate=pl.CostEstimate(
            flops=6 * all_rows * features * width + 4 * all_rows * rows * width,
            bytes_accessed=6 * features * width + 8 * all_rows * width + 2 * all_rows * features,
            transcendentals=all_rows * rows * width // HEAD,
        ),
        name="forward",
    )(hidden, weight, mask)


def backward_kernel(
    upstream_ref, out_ref, weight_ref, qkv_ref, attended_ref, mask_ref, grads_ref, part_ref, total
):
    step = pl.program_id(0)
    d_attended = dot(upstream_ref[...], out_ref[...], NT).astype(jnp.bfloat16)
    mask = mask_ref[...]
    for j in range(weight_ref.shape[2] // HEAD):
        e = pl.ds(j * HEAD, HEAD)
        queries, keys, values = qkv_ref[0, :, e], qkv_ref[1, :, e], qkv_ref[2, :, e]
        d_head = d_attended[:, j * HEAD : (j + 1) * HEAD]
        soft = softmax_of(queries, keys, mask)
        offset = jnp.sum(
            d_head.astype(jnp.float32) * attended_ref[:, e].astype(jnp.float32),
            axis=-1,
            keepdims=True,
        )
        d_probs = dot(d_head, values, NT)
        d_scores = (soft * (d_probs - offset) * HEAD ** (-0.5)).astype(jnp.bfloat16)
        grads_ref[0, :, e] = dot(d_scores, keys).astype(jnp.bfloat16)
        grads_ref[1, :, e] = dot(d_scores, queries, TN).astype(jnp.bfloat16)
        grads_ref[2, :, e] = dot(soft.astype(jnp.bfloat16), d_head, TN).astype(jnp.bfloat16)
    piece = dot(grads_ref[0], weight_ref[0], NT)
    for c in range(1, 3):
        piece = piece + dot(grads_ref[c], weight_ref[c], NT)

    @pl.when(step == 0)
    def _():
        total[...] = piece

    @pl.when(step > 0)
    def _():
        total[...] += piece

    @pl.when(step == pl.num_programs(0) - 1)
    def _():
        part_ref[...] = total[...].astype(jnp.bfloat16)


def backward(tick, upstream, weight_out, weight, qkv, attended, mask):
    rows, features = upstream.shape
    width = weight.shape[2]
    block = 2 * HEAD if width % (2 * HEAD) == 0 else HEAD
    return pl.pallas_call(
        backward_kernel,
        grid=(width // block,),
        in_specs=[
            pl.BlockSpec((rows, features), lambda j: (0, 0)),
            pl.BlockSpec((block, features), lambda j: (j, 0)),
            pl.BlockSpec((3, features, block), lambda j: (0, 0, j)),
            pl.BlockSpec((3, rows, block), lambda j: (0, tick, j)),
            pl.BlockSpec((rows, block), lambda j: (tick, j)),
            pl.BlockSpec((rows, rows), lambda j: (0, 0)),
        ],
        out_specs=[
            pl.BlockSpec((3, rows, block), lambda j: (0, 0, j)),
            pl.BlockSpec((rows, features), lambda j: (0, 0)),
        ],
        out_shape=[
            jax.ShapeDtypeStruct((3, rows, width), jnp.bfloat16),
            jax.ShapeDtypeStruct((rows, features), jnp.bfloat16),
        ],
        scratch_shapes=[pltpu.VMEM((rows, features), jnp.float32)],
        compiler_params=pltpu.CompilerParams(vmem_limit_bytes=VMEM_BYTES),
        cost_estimate=pl.CostEstimate(
            flops=8 * rows * features * width + 12 * rows * rows * width,
            bytes_accessed=8 * features * width + 14 * rows * width + 4 * rows * features,
            transcendentals=rows * rows * width // HEAD,
        ),
        name="backward",
    )(upstream, weight_out, weight, qkv, attended, mask)


def outer_kernel(left_ref, right_ref, out_ref):
    out_ref[0] = dot(left_ref[...], right_ref[0], TN).astype(jnp.bfloat16)


def outer(left, right):
    rows, features = left.shape
    kinds, _, width = right.shape
    block = min(512, features)
    return pl.pallas_call(
        outer_kernel,
        grid=(features // block, kinds),
        in_specs=[
            pl.BlockSpec((rows, block), lambda f, c: (0, f)),
            pl.BlockSpec((1, rows, width), lambda f, c: (c, 0, 0)),
        ],
        out_specs=pl.BlockSpec((1, block, width), lambda f, c: (c, f, 0)),
        out_shape=jax.ShapeDtypeStruct((kinds, features, width), jnp.bfloat16),
        compiler_params=pltpu.CompilerParams(vmem_limit_bytes=VMEM_BYTES),
        cost_estimate=pl.CostEstimate(
            flops=2 * rows * features * width * kinds,
            bytes_accessed=2 * kinds * features * width + 2 * rows * (features + kinds * width),
            transcendentals=0,
        ),
        name="outer",
    )(left, right)


def per_device(
    query_key_value_weight,
    output_weight,
    ascending_query_key_value_weight,
    ascending_output_weight,
    descending_saved_input,
    ascending_saved_input,
    descending_transit_gradient,
    ascending_transit_gradient,
    descending_loss_gradient,
    ascending_loss_gradient,
):
    sections, count = lax.axis_size("section"), lax.axis_size("tp")
    position, place = lax.axis_index("section"), lax.axis_index("tp")
    _, ticks, local_rows, features = descending_saved_input.shape
    rows = local_rows * count
    weight = [
        jnp.transpose(w[0], (1, 0, 2))
        for w in (query_key_value_weight, ascending_query_key_value_weight)
    ]
    weight_out = [output_weight[0], ascending_output_weight[0]]
    normed_down, scale_down = normalize(descending_saved_input[0])
    normed_up, scale_up = normalize(ascending_saved_input[0])
    normed, scale = [normed_down, normed_up], [scale_down, scale_up]
    hidden_own = [n.astype(jnp.bfloat16) for n in normed]
    loss = [descending_loss_gradient, ascending_loss_gradient]
    edge = [position == sections - 1, position == 0]
    steps = [-1, 1]

    index = jnp.arange(rows, dtype=jnp.int32)
    where_from = (place - index // local_rows + count) % count
    true_row = where_from * local_rows + index % local_rows
    mask = (true_row[:, None] >= true_row[None, :]).astype(jnp.float32)

    flow = [descending_transit_gradient[0], ascending_transit_gradient[0]]
    hidden = [gather_rows(h, 1).reshape(ticks * rows, features) for h in hidden_own]
    upstream = [gather_rows(g, 0) for g in flow]
    loss_rows = [gather_rows(g, 1) for g in loss]
    hidden_far_own = mirror(hidden_own[1])
    flow_far_own = [mirror(flow[1])]

    qkv, attended = [None, None], [None, None]
    for pipe in (1, 0):
        qkv[pipe], attended[pipe] = forward(hidden[pipe], weight[pipe], mask)
    attended_far = mirror(attended[1])

    all_upstream, all_grads, grads_far = [], [], []
    departing = [None, None]
    for tick in range(ticks):
        all_upstream.append(upstream[0])
        for pipe in (1, 0):
            grads, part = backward(
                tick, upstream[pipe], weight_out[pipe], weight[pipe], qkv[pipe], attended[pipe], mask
            )
            if pipe == 0:
                all_grads.append(grads)
            else:
                grads_far.append(mirror(grads))
            departing[pipe] = layer_back(
                scatter_rows(part), normed[pipe][tick], scale[pipe][tick], flow[pipe]
            )
        if tick + 1 < ticks:
            for pipe in (1, 0):
                shifted = passed_along(departing[pipe], steps[pipe])
                upstream[pipe] = jnp.where(edge[pipe], loss_rows[pipe][tick], shifted)
                flow[pipe] = upstream[pipe][:local_rows]
            flow_far_own.append(mirror(flow[1]))

    hidden_far = gather_rows(hidden_far_own, 1).reshape(ticks * rows, features)
    upstream_far = [gather_rows(g, 0) for g in flow_far_own]
    grad_out = outer(
        jnp.concatenate([attended[0], attended_far], axis=0),
        jnp.concatenate(all_upstream + upstream_far, axis=0)[None],
    )
    grad_qkv = outer(
        jnp.concatenate([hidden[0], hidden_far], axis=0),
        jnp.concatenate(all_grads + grads_far, axis=1),
    )
    return (
        jnp.transpose(grad_qkv, (1, 0, 2))[None],
        grad_out,
        departing[0][None],
        departing[1][None],
    )


def solution(mesh):
    in_specs = (
        P("section", None, None, "tp"),
        P("section", "tp", None),
        P("section", None, None, "tp"),
        P("section", "tp", None),
        P("section", None, "tp", None),
        P("section", None, "tp", None),
        P("section", "tp", None),
        P("section", "tp", None),
        P(None, "tp", None),
        P(None, "tp", None),
    )
    out_specs = (
        P("section", None, None, "tp"),
        P("section", "tp", None),
        P("section", "tp", None),
        P("section", "tp", None),
    )
    return jax.shard_map(
        per_device, mesh=mesh, in_specs=in_specs, out_specs=out_specs, check_vma=False
    )
```
